32 devices in a mesh: ctx: 16 (over z, y, core), tp: 2 (over x).
Axes of the slice: x: 2, y: 2, z: 4, core: 2. Of those that a mesh axis runs over, the one named last changes fastest.
Arguments:
- q_new: bfloat16 [256, 2048], P(('ctx', 'tp')), may hold values from -128 to 128
- kv_new: bfloat16 [2, 256, 256], P(None, 'ctx', 'tp'), may hold values from -4 to 4
- kv_cache: bfloat16 [2, 7936, 256], P(None, 'ctx', 'tp'), may hold values from -4 to 4
- cache_lens: int32 [16], replicated, may hold values from 1 to 496, 3968 in all
- segment_ids: int32 [256], replicated, may hold values from 0 to 15, never falling along the last dimension, each value on 1 to 32 neighbouring positions
Outputs:
- attn_out: bfloat16 [256, 2048], P(('ctx', 'tp'))
- attn_lse: float32 [256, 16], P('ctx', 'tp')
The draws below stay inside these ranges and needn't reach their ends.
Inputs may be any that keep to these rules, and one draw needn't show every extreme that they name: The filled slots of shard c are its first cache_lens[c] slots; the lengths sum to 3968 and some shard is full. `segment_ids`: never falls along the turn; a segment holds at most 32 tokens, and some segment exactly 32.
All inputs are finite; a program needn't handle non-finite values.
Results may differ from the reference program's by a relative error of at most 0.0015.
Values may be sent and summed in bfloat16 or wider, within the bound.
A program may use at most 64 MiB of HBM per device.

```python
import math
import jax
import jax.numpy as jnp
import numpy as np
from jax import lax

HD = 128
GROUP = 8
CACHE_DEV = 496
QB = 16
KVH = 2
HQ = 16
CACHE = 7936
NEW = 256
N_CTX = 16


def cache_base(key):
    stream = jax.random.fold_in(key, 17)
    base = jnp.clip(jax.random.normal(stream, (2, CACHE, KVH * HD), jnp.float32), -4.0, 4.0)
    return base


def draw_kv_cache(key, part):
    return cache_base(key).astype(jnp.bfloat16)


def draw_q_new(key, part):
    stream = jax.random.fold_in(key, 29)
    base = jnp.clip(3.0 * jax.random.normal(stream, (NEW, HQ * HD), jnp.float32), -18.0, 18.0)
    return base.astype(jnp.bfloat16)


def levels(own_key, dims, cuts, smallest, top_value):
    def one(axis_at, shards_of):
        draws = jax.random.uniform(jax.random.fold_in(jax.random.fold_in(own_key, 6), axis_at), (shards_of,), jnp.float32, smallest / len(cuts), top_value / len(cuts))
        return jnp.repeat(jnp.exp(draws), dims[axis_at] // shards_of).reshape((-1,) + (1,) * (len(dims) - axis_at - 1))

    level = one(*cuts[0])
    for cut in cuts[1:]:
        level = level * one(*cut)
    return level


def length_profile(amount, total, reach, slope):
    weights = [(1 << 20) // math.isqrt(standing ** slope) + 1 for standing in range(2, amount + 1)]
    rest, holding = total - reach - (amount - 1), [1] * (amount - 1)
    while rest > 0:
        free = [i for i in range(amount - 1) if holding[i] < reach]
        whole, budget = sum([weights[i] for i in free]), rest
        for i in free:
            addition = min(reach - holding[i], max(1, budget * weights[i] // whole), rest)
            holding[i] = holding[i] + addition
            rest = rest - addition
    return np.array([reach] + holding)


def uneven_parts(key, amount, total, reach, slope):
    if amount == 2:
        one = jax.random.randint(key, (), max(1, total - reach), min(reach, total - 1) + 1)
        return jnp.stack([one, total - one])
    sizes = jnp.asarray(length_profile(amount, total, reach, slope), jnp.int32)
    couples = (amount - 1) // 2
    source_of, taker = sizes[1:1 + 2 * couples:2], sizes[2:2 + 2 * couples:2]
    room = jnp.minimum(source_of - 1, reach - taker)
    shifted = jax.random.randint(jax.random.fold_in(key, 1), (couples,), 0, 1 << 20) % (room + 1)
    sizes = sizes.at[1:1 + 2 * couples:2].set(source_of - shifted).at[2:2 + 2 * couples:2].set(taker + shifted)
    return sizes[jax.random.permutation(jax.random.fold_in(key, 2), amount)]


def bell_draw(rng, dims, spread, bound, split=(), kind=jnp.bfloat16):
    entries = jax.random.normal(rng, dims, jnp.float32) * spread
    if len(split) > 0:
        entries = levels(rng, dims, split, -0.22, 0.18) * entries
    return jnp.clip(entries, min=-bound, max=bound).astype(kind)


def setup_inputs(seed: int = 0) -> dict:
    splits = jax.random.split(jax.random.key(seed), 6)
    q_new = draw_q_new(jax.random.fold_in(splits[5], 71), 0)
    kv_new = bell_draw(splits[1], (2, NEW, KVH * HD), 1.0, 4.0, ((1, 16), (2, 2)))
    kv_cache = draw_kv_cache(jax.random.fold_in(splits[5], 71), 0)
    cache_lens = uneven_parts(splits[3], N_CTX, CACHE // 2, CACHE_DEV, 2).astype(jnp.int32)
    segment_ids = jnp.searchsorted(jnp.cumsum(uneven_parts(splits[4], NEW // 16, NEW, 32, 2)), jnp.arange(NEW), side="right").astype(jnp.int32)
    return {"q_new": q_new, "kv_new": kv_new, "kv_cache": kv_cache, "cache_lens": cache_lens, "segment_ids": segment_ids}


def shard_partial(queries, query_seg, keys_all, values_all, filled, key_seg, head_dim):
    rows = queries.shape[0]
    heads = queries.shape[1] // head_dim
    total = keys_all.shape[0]
    cache_count = total - key_seg.shape[0]
    flat = queries.reshape(rows * heads, head_dim)
    scores = jnp.dot(flat, keys_all.T, preferred_element_type=jnp.float32) * (head_dim ** -0.5)
    scores = scores.reshape(rows, heads, total)
    slot_rank = jnp.where(jnp.arange(cache_count) < filled, -1, 2 ** 30).astype(jnp.int32)
    key_rank = jnp.concatenate([slot_rank, key_seg.astype(jnp.int32)])
    visible = key_rank[None, None, :] <= query_seg.astype(jnp.int32)[:, None, None]
    masked = jnp.where(visible, scores, -jnp.inf)
    peak = jnp.max(masked, axis=2)
    expo = jnp.exp(masked - peak[:, :, None])
    denom = jnp.sum(expo, axis=2)
    weights = expo.astype(jnp.bfloat16).reshape(rows * heads, total)
    mixed = jnp.dot(weights, values_all, preferred_element_type=jnp.float32)
    mixed = mixed.reshape(rows, heads, head_dim) / denom[:, :, None]
    return mixed.reshape(rows, heads * head_dim), peak + jnp.log(denom)


def reference(q_new, kv_new, kv_cache, cache_lens, segment_ids):
    outputs = []
    totals = []
    for group in range(KVH):
        lo = group * HD
        queries = q_new[:, group * GROUP * HD:(group + 1) * GROUP * HD]
        cache_keys = kv_cache[0, :, lo:lo + HD]
        cache_values = kv_cache[1, :, lo:lo + HD]
        new_keys = kv_new[0, :, lo:lo + HD]
        new_values = kv_new[1, :, lo:lo + HD]

        def visit(carry, shard):
            peak_run, denom_run, numer_run = carry
            start = (shard * CACHE_DEV).astype(jnp.int32)
            begin = (shard * QB).astype(jnp.int32)
            keys_all = jnp.concatenate([lax.dynamic_slice_in_dim(cache_keys, start, CACHE_DEV, 0), lax.dynamic_slice_in_dim(new_keys, begin, QB, 0)])
            values_all = jnp.concatenate([lax.dynamic_slice_in_dim(cache_values, start, CACHE_DEV, 0), lax.dynamic_slice_in_dim(new_values, begin, QB, 0)])
            key_seg = lax.dynamic_slice_in_dim(segment_ids, begin, QB, 0)
            mixed, lse = shard_partial(queries, segment_ids, keys_all, values_all, cache_lens[shard], key_seg, HD)
            peak = jnp.maximum(peak_run, lse)
            keep = jnp.exp(peak_run - peak)
            fresh = jnp.exp(lse - peak)
            numer = numer_run * keep[:, :, None] + mixed.reshape(NEW, GROUP, HD) * fresh[:, :, None]
            return (peak, denom_run * keep + fresh, numer), None

        init = (jnp.full((NEW, GROUP), -jnp.inf, jnp.float32), jnp.zeros((NEW, GROUP), jnp.float32), jnp.zeros((NEW, GROUP, HD), jnp.float32))
        (peak, denom, numer), _ = lax.scan(visit, init, jnp.arange(N_CTX, dtype=jnp.int32))
        outputs.append((numer / denom[:, :, None]).reshape(NEW, GROUP * HD).astype(jnp.bfloat16))
        totals.append(peak + jnp.log(denom))
    return jnp.concatenate(outputs, axis=1), jnp.concatenate(totals, axis=1)
```

```python
import functools
import math

import jax
import jax.numpy as jnp
from jax import lax
from jax.experimental import pallas as pl
from jax.experimental.pallas import tpu as pltpu
from jax.sharding import PartitionSpec as P

GANG = 4


def kernel(
    H, T, R, scale,
    q_ref, cache_ref, new_ref, lens_ref, end_ref,
    out_ref, lse_ref,
    qbuf, kv, osend, orecv, acc, run, wcol, lsebuf,
    q_send, q_recv, kv_send, kv_recv, own_sem, o_send, o_recv,
):
    c2 = scale * math.log2(math.e)
    ctx, me = lax.axis_index("ctx"), lax.axis_index("tp")
    hi, lo = ctx // GANG, lax.rem(ctx, GANG)
    base = hi * GANG
    b0, b1 = lax.rem(lo, 2), lo // 2
    flip = [b1 * 2 + b0, b1 * 2 + 1 - b0, (1 - b1) * 2 + b0, (1 - b1) * 2 + 1 - b0]
    slots, block = cache_ref.shape[1], new_ref.shape[1]
    keys = slots + block

    def dev(c, t):
        return {"ctx": c, "tp": t}

    def peer(j):
        return lax.rem(hi + j + H, H) * GANG + lo

    def tpeer(i):
        return lax.rem(me + i + T, T)

    barrier = pltpu.get_barrier_semaphore()
    count = 0
    for j in range(H):
        for i in range(T):
            if j or i:
                pl.semaphore_signal(barrier, inc=1, device_id=dev(peer(j), tpeer(i)))
                count += 1
    for r in (1, 2):
        pl.semaphore_signal(barrier, inc=1, device_id=dev(base + flip[r], me))
        count += 1
    own = [
        pltpu.make_async_copy(cache_ref, kv.at[0, :, 0:slots], own_sem.at[0]),
        pltpu.make_async_copy(new_ref, kv.at[0, :, slots:keys], own_sem.at[1]),
    ]
    for copy in own:
        copy.start()
    pl.semaphore_wait(barrier, count)

    def kv_copies(r):
        target = dev(base + flip[r], me)
        return [
            pltpu.make_async_remote_copy(
                cache_ref, kv.at[r, :, 0:slots], kv_send.at[r, 0], kv_recv.at[r, 0], device_id=target),
            pltpu.make_async_remote_copy(
                new_ref, kv.at[r, :, slots:keys], kv_send.at[r, 1], kv_recv.at[r, 1], device_id=target),
        ]

    def q_copy(j, i):
        g = tpeer(i)
        return pltpu.make_async_remote_copy(
            q_ref.at[g], qbuf.at[j, me], q_send.at[j, i], q_recv.at[j, i],
            device_id=dev(peer(-j), g))

    def q_arrival(j, i):
        return pltpu.make_async_remote_copy(
            q_ref.at[me], qbuf.at[j, tpeer(-i)], q_send.at[j, i], q_recv.at[j, i],
            device_id=dev(peer(j), tpeer(-i)))

    far, near = kv_copies(2), kv_copies(1)
    for j in range(H):
        for i in range(T):
            if j or i:
                q_copy(j, i).start()
    for copy in far + near:
        copy.start()
    qbuf[0, me] = q_ref[me]
    for j in range(H):
        for i in range(T):
            if j or i:
                q_arrival(j, i).wait_recv()
    for copy in own:
        copy.wait()

    relay = pltpu.make_async_remote_copy(
        kv.at[2], kv.at[3], kv_send.at[3, 0], kv_recv.at[3, 0], device_id=dev(base + flip[1], me))

    def o_copy(j, i):
        t = tpeer(i)
        return pltpu.make_async_remote_copy(
            osend.at[j, t], orecv.at[j, me], o_send.at[j, i], o_recv.at[j, i],
            device_id=dev(peer(j), t))

    def o_arrival(j, i):
        return pltpu.make_async_remote_copy(
            osend.at[j, me], orecv.at[j, tpeer(-i)], o_send.at[j, i], o_recv.at[j, i],
            device_id=dev(peer(-j), tpeer(-i)))

    B = T * R
    group = 2 if H % 2 == 0 else 1
    width = group * B
    for r in range(GANG):
        if r == 1:
            for copy in near:
                copy.wait_recv()
        if r == 2:
            for copy in far:
                copy.wait_recv()
            relay.start()
        if r == 3:
            relay.wait_recv()
        shard = base + flip[r]
        filled = lens_ref[shard]
        for u in range(H // group):
            queries = qbuf[u * group:(u + 1) * group].reshape(width, q_ref.shape[2])
            ends = jnp.concatenate(
                [end_ref[pl.ds(peer(u * group + k), 1), :] for k in range(group)], axis=1)
            scores = lax.dot_general(
                kv[r, 0], queries, (((1,), (1,)), ((), ())), preferred_element_type=jnp.float32)
            old = scores[0:slots]
            spot = lax.broadcasted_iota(jnp.int32, old.shape, 0)
            old = jnp.where(spot < filled, old, -jnp.inf)
            fresh = scores[slots:keys]
            place = lax.broadcasted_iota(jnp.int32, fresh.shape, 0) + shard * block
            fresh = jnp.where(place < ends, fresh, -jnp.inf)
            masked = jnp.concatenate([old, fresh], axis=0)
            peak = jnp.max(masked, axis=0, keepdims=True)
            expo = jnp.exp2((masked - peak) * c2)
            total = jnp.sum(expo, axis=0, keepdims=True)
            mixed = lax.dot_general(
                kv[r, 1], expo.astype(jnp.bfloat16), (((0,), (0,)), ((), ())),
                preferred_element_type=jnp.float32)
            if r == 0:
                top, denom, numer = peak, total, mixed
            else:
                before = run[u, 0:1]
                top = jnp.maximum(before, peak)
                keep, add = jnp.exp2((before - top) * c2), jnp.exp2((peak - top) * c2)
                denom = run[u, 1:2] * keep + total * add
                numer = acc[u] * keep + mixed * add
            if r < GANG - 1:
                run[u, 0:1], run[u, 1:2] = top, denom
                acc[u] = numer
            else:
                rows = numer.T.reshape(group, T, R, q_ref.shape[2])
                for k in range(group):
                    j = u * group + k
                    osend[j, :, 0:R] = rows[k]
                    tops = jnp.broadcast_to(top[:, k * B:(k + 1) * B], (4, B))
                    denoms = jnp.broadcast_to(denom[:, k * B:(k + 1) * B], (4, B))
                    tail = jnp.concatenate([tops, denoms], axis=0)
                    for t in range(T):
                        osend[j, t, R:R + 8] = tail
                    for i in range(T):
                        if j or i:
                            o_copy(j, i).start()
    orecv[0, me] = osend[0, me]
    for j in range(H):
        for i in range(T):
            if j or i:
                o_arrival(j, i).wait_recv()
    for g in range(T):
        tops = [orecv[j, g, R:R + 1] for j in range(H)]
        top = functools.reduce(jnp.maximum, tops)
        ws = [jnp.exp2((x - top) * c2) for x in tops]
        total = sum(w * orecv[j, g, R + 4:R + 5] for j, w in enumerate(ws))
        lsebuf[g] = jnp.broadcast_to(top * scale + jnp.log(total), (8, B))
        inverse = 1.0 / total
        ws = [w * inverse for w in ws]
        ws += [jnp.zeros_like(top)] * (-H % 8)
        wcol[...] = jnp.concatenate(ws, axis=0).T
        cols = wcol[pl.ds(me * R, R), :]
        final = sum(cols[:, j:j + 1] * orecv[j, g, 0:R] for j in range(H))
        out_ref[g] = final.astype(out_ref.dtype)
    lse_ref[...] = lsebuf[me]
    for j in range(H):
        for i in range(T):
            if j or i:
                q_copy(j, i).wait_send()
                o_copy(j, i).wait_send()
    for copy in far + near + [relay]:
        copy.wait_send()


def shards(q_new, kv_new, kv_cache, cache_lens, segment_ids):
    hd = kv_cache.shape[2]
    block, slots = kv_new.shape[1], kv_cache.shape[1]
    tokens = q_new.shape[0]
    n, T = lax.axis_size("ctx"), lax.axis_size("tp")
    H = n // GANG
    heads = q_new.shape[1] // (hd * T)
    R = tokens * heads
    B = T * R
    hpad = H + (-H % 8)
    q = q_new.reshape(tokens, T, heads, hd).transpose(1, 0, 2, 3).reshape(T, R, hd)
    ends = jnp.sum((segment_ids[None, :] <= segment_ids[:, None]).astype(jnp.int32), axis=1)
    ends = jnp.repeat(ends, heads).reshape(n, B)
    vmem = pl.BlockSpec(memory_space=pltpu.VMEM)
    hbm = pl.BlockSpec(memory_space=pl.ANY)
    dma = pltpu.SemaphoreType.DMA
    out, lse = pl.pallas_call(
        functools.partial(kernel, H, T, R, hd ** -0.5),
        out_shape=(
            jax.ShapeDtypeStruct((T, R, hd), jnp.bfloat16),
            jax.ShapeDtypeStruct((8, B), jnp.float32),
        ),
        in_specs=[vmem, hbm, hbm, pl.BlockSpec(memory_space=pltpu.SMEM), vmem],
        out_specs=(vmem, vmem),
        scratch_shapes=[
            pltpu.VMEM((H, T, R, hd), jnp.bfloat16),
            pltpu.VMEM((GANG, 2, slots + block, hd), jnp.bfloat16),
            pltpu.VMEM((H, T, R + 8, hd), jnp.float32),
            pltpu.VMEM((H, T, R + 8, hd), jnp.float32),
            pltpu.VMEM((H // 2 if H % 2 == 0 else H, hd, 2 * B if H % 2 == 0 else B), jnp.float32),
            pltpu.VMEM((H // 2 if H % 2 == 0 else H, 8, 2 * B if H % 2 == 0 else B), jnp.float32),
            pltpu.VMEM((B, hpad), jnp.float32),
            pltpu.VMEM((T, 8, B), jnp.float32),
            dma((H, T)), dma((H, T)), dma((GANG, 2)), dma((GANG, 2)), dma((2,)), dma((H, T)), dma((H, T)),
        ],
        compiler_params=pltpu.CompilerParams(
            collective_id=0, has_side_effects=True, vmem_limit_bytes=48 * 2 ** 20),
    )(q, kv_cache, kv_new, cache_lens, ends)
    attn = out.reshape(T, tokens, heads, hd).transpose(1, 0, 2, 3).reshape(tokens, T * heads * hd)
    return attn, lse[0].reshape(block, heads)


def solution(mesh):
    return jax.shard_map(
        shards,
        mesh=mesh,
        in_specs=(P(("ctx", "tp"), None), P(None, "ctx", "tp"), P(None, "ctx", "tp"), P(), P()),
        out_specs=(P(("ctx", "tp"), None), P("ctx", "tp")),
        check_vma=False,
    )
```

```python
import functools
import math

import jax
import jax.numpy as jnp
from jax import lax
from jax.experimental import pallas as pl
from jax.experimental.pallas import tpu as pltpu
from jax.sharding import PartitionSpec as P

TINY, STEPS = 1e-30, 32767.0
GANG = 4


def kernel(
    H, T, R, scale,
    q_hbm, cache_ref, new_ref, lens_hbm, seg_hbm,
    out_ref, lse_ref,
    qraw, q_ref, lens_ref, segrow, segcol, qseg,
    qbuf, kv, osend, orecv, ssend, srecv, acc, run, wcol, lsebuf,
    q_send, q_recv, kv_send, kv_recv, own_sem, o_send, o_recv, s_send, s_recv,
):
    c2 = scale * math.log2(math.e)
    ctx, me = lax.axis_index("ctx"), lax.axis_index("tp")
    hi, lo = ctx // GANG, lax.rem(ctx, GANG)
    base = hi * GANG
    b0, b1 = lax.rem(lo, 2), lo // 2
    flip = [b1 * 2 + b0, b1 * 2 + 1 - b0, (1 - b1) * 2 + b0, (1 - b1) * 2 + 1 - b0]
    slots, block = cache_ref.shape[1], new_ref.shape[1]
    keys = slots + block
    tokens, hd = qraw.shape[0], cache_ref.shape[2]
    heads, B = R // tokens, T * R

    def dev(c, t):
        return {"ctx": c, "tp": t}

    def peer(j):
        return lax.rem(hi + j + H, H) * GANG + lo

    def tpeer(i):
        return lax.rem(me + i + T, T)

    barrier = pltpu.get_barrier_semaphore()
    count = 0
    for j in range(H):
        for i in range(T):
            if j or i:
                pl.semaphore_signal(barrier, inc=1, device_id=dev(peer(j), tpeer(i)))
                count += 1
    for r in (1, 2):
        pl.semaphore_signal(barrier, inc=1, device_id=dev(base + flip[r], me))
        count += 1
    local = [
        pltpu.make_async_copy(q_hbm, qraw, own_sem.at[0]),
        pltpu.make_async_copy(seg_hbm, segrow, own_sem.at[1]),
        pltpu.make_async_copy(lens_hbm, lens_ref, own_sem.at[2]),
        pltpu.make_async_copy(new_ref, kv.at[0, :, slots:keys], own_sem.at[3]),
        pltpu.make_async_copy(cache_ref, kv.at[0, :, 0:slots], own_sem.at[4]),
    ]
    for copy in local:
        copy.start()
    local[0].wait()
    for g in range(T):
        first = g * heads * hd
        wide = qraw[:, first:first + heads * hd].astype(jnp.float32)
        q_ref[g] = jnp.concatenate(
            [wide[:, h * hd:(h + 1) * hd] for h in range(heads)], axis=0).astype(jnp.bfloat16)
    local[1].wait()
    total_new = segrow.shape[1]
    segcol[...] = jnp.broadcast_to(segrow[...].astype(jnp.float32), (8, total_new)).T
    lane = lax.broadcasted_iota(jnp.int32, (1, B), 1)
    inside = lax.div(lane, jnp.int32(R)) * tokens + lax.rem(lane, jnp.int32(tokens))
    token = lax.broadcasted_iota(jnp.int32, (total_new, B), 0)
    for j in range(H):
        here = token == inside + peer(j) * block
        qseg[j:j + 1] = jnp.sum(jnp.where(here, segcol[:, 0:1], 0.0), axis=0, keepdims=True)
    for copy in local[2:]:
        copy.wait()
    pl.semaphore_wait(barrier, count)

    def q_copy(j, i):
        g = tpeer(i)
        return pltpu.make_async_remote_copy(
            q_ref.at[g], qbuf.at[j, me], q_send.at[j, i], q_recv.at[j, i],
            device_id=dev(peer(-j), g))

    def q_arrival(j, i):
        return pltpu.make_async_remote_copy(
            q_ref.at[me], qbuf.at[j, tpeer(-i)], q_send.at[j, i], q_recv.at[j, i],
            device_id=dev(peer(j), tpeer(-i)))

    def kv_copy(source, slot, part, hop):
        return pltpu.make_async_remote_copy(
            kv.at[source, part], kv.at[slot, part], kv_send.at[slot, part], kv_recv.at[slot, part],
            device_id=dev(base + flip[hop], me))

    far = [kv_copy(0, 2, part, 2) for part in range(2)]
    near = [kv_copy(0, 1, part, 1) for part in range(2)]
    relay = [kv_copy(2, 3, part, 1) for part in range(2)]
    for j in range(H):
        for i in range(T):
            if j or i:
                q_copy(j, i).start()
    for copy in far + near:
        copy.start()
    qbuf[0, me] = q_ref[me]
    for j in range(H):
        for i in range(T):
            if j or i:
                q_arrival(j, i).wait_recv()

    def o_copy(j, i):
        t = tpeer(i)
        return pltpu.make_async_remote_copy(
            osend.at[j, t], orecv.at[j, me], o_send.at[j, i], o_recv.at[j, i],
            device_id=dev(peer(j), t))

    def o_arrival(j, i):
        return pltpu.make_async_remote_copy(
            osend.at[j, me], orecv.at[j, tpeer(-i)], o_send.at[j, i], o_recv.at[j, i],
            device_id=dev(peer(-j), tpeer(-i)))

    def s_copy(j, i):
        return pltpu.make_async_remote_copy(
            ssend.at[j], srecv.at[j, me], s_send.at[j, i], s_recv.at[j, i],
            device_id=dev(peer(j), tpeer(i)))

    def s_arrival(j, i):
        return pltpu.make_async_remote_copy(
            ssend.at[j], srecv.at[j, tpeer(-i)], s_send.at[j, i], s_recv.at[j, i],
            device_id=dev(peer(-j), tpeer(-i)))

    group = 2 if H % 2 == 0 else 1
    width = group * B
    for r in range(GANG):
        if r == 1:
            for copy in near:
                copy.wait_recv()
        if r == 2:
            for copy, onward in zip(far, relay):
                copy.wait_recv()
                onward.start()
        if r == 3:
            for copy in relay:
                copy.wait_recv()
        shard = base + flip[r]
        filled = lens_ref[shard]
        for u in range(H // group):
            queries = qbuf[u * group:(u + 1) * group].reshape(width, q_ref.shape[2])
            asks = jnp.concatenate(
                [qseg[u * group + k:u * group + k + 1] for k in range(group)], axis=1)
            scores = lax.dot_general(
                kv[r, 0], queries, (((1,), (1,)), ((), ())), preferred_element_type=jnp.float32)
            old = scores[0:slots]
            spot = lax.broadcasted_iota(jnp.int32, old.shape, 0)
            old = jnp.where(spot < filled, old, -jnp.inf)
            fresh = scores[slots:keys]
            theirs = segcol[pl.ds(pl.multiple_of(shard * block, block), block), 0:1]
            fresh = jnp.where(theirs <= asks, fresh, -jnp.inf)
            masked = jnp.concatenate([old, fresh], axis=0)
            peak = jnp.max(masked, axis=0, keepdims=True)
            expo = jnp.exp2((masked - peak) * c2)
            total = jnp.sum(expo, axis=0, keepdims=True)
            mixed = lax.dot_general(
                kv[r, 1], expo.astype(jnp.bfloat16), (((0,), (0,)), ((), ())),
                preferred_element_type=jnp.float32)
            if r == 0:
                top, denom, numer = peak, total, mixed
            else:
                before = run[u, 0:1]
                top = jnp.maximum(before, peak)
                keep, add = jnp.exp2((before - top) * c2), jnp.exp2((peak - top) * c2)
                denom = run[u, 1:2] * keep + total * add
                numer = acc[u] * keep + mixed * add
            if r < GANG - 1:
                run[u, 0:1], run[u, 1:2] = top, denom
                acc[u] = numer
            else:
                most = jnp.maximum(jnp.max(jnp.abs(numer), axis=0, keepdims=True), TINY)
                level = jnp.round(numer * (STEPS / most))
                rows = level.T.astype(jnp.int32).astype(jnp.int16).reshape(group, T, R, hd)
                for k in range(group):
                    j = u * group + k
                    osend[j] = rows[k]
                    stats = [x[:, k * B:(k + 1) * B] for x in (top, denom, most)]
                    ssend[j] = jnp.concatenate(stats + stats[:1] * 5, axis=0)
                    for i in range(T):
                        if j or i:
                            s_copy(j, i).start()
                            o_copy(j, i).start()
    orecv[0, me] = osend[0, me]
    srecv[0, me] = ssend[0]
    for j in range(H):
        for i in range(T):
            if j or i:
                s_arrival(j, i).wait_recv()
                o_arrival(j, i).wait_recv()
    for g in range(T):
        tops = [srecv[j, g, 0:1] for j in range(H)]
        top = functools.reduce(jnp.maximum, tops)
        ws = [jnp.exp2((x - top) * c2) for x in tops]
        total = sum(w * srecv[j, g, 1:2] for j, w in enumerate(ws))
        lsebuf[g] = jnp.broadcast_to(top * scale + jnp.log(total), (8, B))
        inverse = 1.0 / (total * STEPS)
        ws = [w * srecv[j, g, 2:3] * inverse for j, w in enumerate(ws)]
        ws += [jnp.zeros_like(top)] * (-H % 8)
        wcol[...] = jnp.concatenate(ws, axis=0).T
        cols = wcol[pl.ds(me * R, R), :]
        final = sum(
            cols[:, j:j + 1] * orecv[j, g].astype(jnp.int32).astype(jnp.float32) for j in range(H))
        first = g * heads * hd
        out_ref[:, first:first + heads * hd] = jnp.concatenate(
            [final[h * tokens:(h + 1) * tokens] for h in range(heads)], axis=1).astype(out_ref.dtype)
    lse_ref[...] = lsebuf[me]
    for j in range(H):
        for i in range(T):
            if j or i:
                q_copy(j, i).wait_send()
                s_copy(j, i).wait_send()
                o_copy(j, i).wait_send()
    for copy in far + near + relay:
        copy.wait_send()


def shards(q_new, kv_new, kv_cache, cache_lens, segment_ids):
    hd = kv_cache.shape[2]
    block, slots = kv_new.shape[1], kv_cache.shape[1]
    tokens = q_new.shape[0]
    n, T = lax.axis_size("ctx"), lax.axis_size("tp")
    H = n // GANG
    heads = q_new.shape[1] // (hd * T)
    R = tokens * heads
    B = T * R
    hpad = H + (-H % 8)
    vmem = pl.BlockSpec(memory_space=pltpu.VMEM)
    hbm = pl.BlockSpec(memory_space=pltpu.HBM)
    group = 2 if H % 2 == 0 else 1
    new = segment_ids.shape[0]
    dma = pltpu.SemaphoreType.DMA
    out, lse = pl.pallas_call(
        functools.partial(kernel, H, T, R, hd ** -0.5),
        out_shape=(
            jax.ShapeDtypeStruct(q_new.shape, jnp.bfloat16),
            jax.ShapeDtypeStruct((8, B), jnp.float32),
        ),
        in_specs=[hbm] * 5,
        out_specs=(vmem, vmem),
        scratch_shapes=[
            pltpu.VMEM(q_new.shape, jnp.bfloat16),
            pltpu.VMEM((T, R, hd), jnp.bfloat16),
            pltpu.SMEM(cache_lens.shape, jnp.int32),
            pltpu.VMEM((1, new), jnp.int32),
            pltpu.VMEM((new, 8), jnp.float32),
            pltpu.VMEM((H, B), jnp.float32),
            pltpu.VMEM((H, T, R, hd), jnp.bfloat16),
            pltpu.VMEM((GANG, 2, slots + block, hd), jnp.bfloat16),
            pltpu.VMEM((H, T, R, hd), jnp.int16),
            pltpu.VMEM((H, T, R, hd), jnp.int16),
            pltpu.VMEM((H, 8, B), jnp.float32),
            pltpu.VMEM((H, T, 8, B), jnp.float32),
            pltpu.VMEM((H // group, hd, group * B), jnp.float32),
            pltpu.VMEM((H // group, 8, group * B), jnp.float32),
            pltpu.VMEM((B, hpad), jnp.float32),
            pltpu.VMEM((T, 8, B), jnp.float32),
            dma((H, T)), dma((H, T)), dma((GANG, 2)), dma((GANG, 2)), dma((5,)), dma((H, T)), dma((H, T)), dma((H, T)), dma((H, T)),
        ],
        compiler_params=pltpu.CompilerParams(
            collective_id=0, has_side_effects=True, vmem_limit_bytes=48 * 2 ** 20),
    )(q_new, kv_cache, kv_new, cache_lens, segment_ids.reshape(1, new))
    lse = lse[0].reshape(T, heads, tokens).transpose(0, 2, 1).reshape(block, heads)
    return out, lse


def solution(mesh):
    return jax.shard_map(
        shards,
        mesh=mesh,
        in_specs=(P(("ctx", "tp"), None), P(None, "ctx", "tp"), P(None, "ctx", "tp"), P(), P()),
        out_specs=(P(("ctx", "tp"), None), P("ctx", "tp")),
        check_vma=False,
    )
```

```python
import functools
import math

import jax
import jax.numpy as jnp
from jax import lax
from jax.experimental import pallas as pl
from jax.experimental.pallas import tpu as pltpu
from jax.sharding import PartitionSpec as P

TINY, STEPS = 1e-30, 32767.0
GANG = 4


def kernel(
    H, T, R, scale,
    q_hbm, cache_ref, new_ref, lens_hbm, seg_hbm,
    out_ref, lse_ref,
    qraw, q_ref, lens_ref, segrow, segcol, qseg,
    qbuf, kv, osend, orecv, ssend, srecv, acc, run, wcol, lsebuf,
    q_send, q_recv, kv_send, kv_recv, own_sem, o_send, o_recv, s_send, s_recv,
):
    c2 = scale * math.log2(math.e)
    ctx, me = lax.axis_index("ctx"), lax.axis_index("tp")
    hi, lo = ctx // GANG, lax.rem(ctx, GANG)
    base = hi * GANG
    b0, b1 = lax.rem(lo, 2), lo // 2
    flip = [b1 * 2 + b0, b1 * 2 + 1 - b0, (1 - b1) * 2 + b0, (1 - b1) * 2 + 1 - b0]
    slots, block = cache_ref.shape[1], new_ref.shape[1]
    keys = slots + block
    tokens, hd = qraw.shape[0], cache_ref.shape[2]
    heads, B = R // tokens, T * R

    def dev(c, t):
        return {"ctx": c, "tp": t}

    def peer(j):
        return lax.rem(hi + j + H, H) * GANG + lo

    def tpeer(i):
        return lax.rem(me + i + T, T)

    barrier = pltpu.get_barrier_semaphore()
    count = 0
    for j in range(H):
        for i in range(T):
            if j or i:
                pl.semaphore_signal(barrier, inc=1, device_id=dev(peer(j), tpeer(i)))
                count += 1
    for r in (1, 2):
        pl.semaphore_signal(barrier, inc=1, device_id=dev(base + flip[r], me))
        count += 1
    local = [
        pltpu.make_async_copy(q_hbm, qraw, own_sem.at[0]),
        pltpu.make_async_copy(seg_hbm, segrow, own_sem.at[1]),
        pltpu.make_async_copy(lens_hbm, lens_ref, own_sem.at[2]),
        pltpu.make_async_copy(new_ref, kv.at[0, :, slots:keys], own_sem.at[3]),
        pltpu.make_async_copy(cache_ref, kv.at[0, :, 0:slots], own_sem.at[4]),
    ]
    for copy in local:
        copy.start()
    local[0].wait()
    for g in range(T):
        first = g * heads * hd
        wide = qraw[:, first:first + heads * hd].astype(jnp.float32)
        q_ref[g] = jnp.concatenate(
            [wide[:, h * hd:(h + 1) * hd] for h in range(heads)], axis=0).astype(jnp.bfloat16)
    local[1].wait()
    total_new = segrow.shape[1]
    segcol[...] = jnp.broadcast_to(segrow[...].astype(jnp.float32), (8, total_new)).T
    lane = lax.broadcasted_iota(jnp.int32, (1, B), 1)
    inside = lax.div(lane, jnp.int32(R)) * tokens + lax.rem(lane, jnp.int32(tokens))
    token = lax.broadcasted_iota(jnp.int32, (total_new, B), 0)
    for j in range(H):
        here = token == inside + peer(j) * block
        qseg[j:j + 1] = jnp.sum(jnp.where(here, segcol[:, 0:1], 0.0), axis=0, keepdims=True)
    for copy in local[2:]:
        copy.wait()
    pl.semaphore_wait(barrier, count)

    def q_copy(j, i):
        g = tpeer(i)
        return pltpu.make_async_remote_copy(
            q_ref.at[g], qbuf.at[j, me], q_send.at[j, i], q_recv.at[j, i],
            device_id=dev(peer(-j), g))

    def q_arrival(j, i):
        return pltpu.make_async_remote_copy(
            q_ref.at[me], qbuf.at[j, tpeer(-i)], q_send.at[j, i], q_recv.at[j, i],
            device_id=dev(peer(j), tpeer(-i)))

    def kv_copy(source, slot, part, hop):
        return pltpu.make_async_remote_copy(
            kv.at[source, part], kv.at[slot, part], kv_send.at[slot, part], kv_recv.at[slot, part],
            device_id=dev(base + flip[hop], me))

    far = [kv_copy(0, 2, part, 2) for part in range(2)]
    near = [kv_copy(0, 1, part, 1) for part in range(2)]
    relay = [kv_copy(2, 3, part, 1) for part in range(2)]
    for j in range(H):
        for i in range(T):
            if j or i:
                q_copy(j, i).start()
    for copy in far + near:
        copy.start()
    qbuf[0, me] = q_ref[me]
    for j in range(H):
        for i in range(T):
            if j or i:
                q_arrival(j, i).wait_recv()

    def o_copy(j, i):
        t = tpeer(i)
        return pltpu.make_async_remote_copy(
            osend.at[j, t], orecv.at[j, me], o_send.at[j, i], o_recv.at[j, i],
            device_id=dev(peer(j), t))

    def o_arrival(j, i):
        return pltpu.make_async_remote_copy(
            osend.at[j, me], orecv.at[j, tpeer(-i)], o_send.at[j, i], o_recv.at[j, i],
            device_id=dev(peer(-j), tpeer(-i)))

    def s_copy(j, i):
        return pltpu.make_async_remote_copy(
            ssend.at[j], srecv.at[j, me], s_send.at[j, i], s_recv.at[j, i],
            device_id=dev(peer(j), tpeer(i)))

    def s_arrival(j, i):
        return pltpu.make_async_remote_copy(
            ssend.at[j], srecv.at[j, tpeer(-i)], s_send.at[j, i], s_recv.at[j, i],
            device_id=dev(peer(-j), tpeer(-i)))

    group = 2 if H % 2 == 0 else 1
    width = group * B
    units = H // group
    order = [(r, u) for r in (0, 1) for u in range(units)] + [(r, u) for u in range(units) for r in (2, 3)]
    for r, u in order:
        if u == 0:
            if r == 1:
                for copy in near:
                    copy.wait_recv()
            if r == 2:
                for copy, onward in zip(far, relay):
                    copy.wait_recv()
                    onward.start()
            if r == 3:
                for copy in relay:
                    copy.wait_recv()
        shard = base + flip[r]
        filled = lens_ref[shard]
        queries = qbuf[u * group:(u + 1) * group].reshape(width, q_ref.shape[2])
        asks = jnp.concatenate(
            [qseg[u * group + k:u * group + k + 1] for k in range(group)], axis=1)
        scores = lax.dot_general(
            kv[r, 0], queries, (((1,), (1,)), ((), ())), preferred_element_type=jnp.float32)
        old = scores[0:slots]
        spot = lax.broadcasted_iota(jnp.int32, old.shape, 0)
        old = jnp.where(spot < filled, old, -jnp.inf)
        fresh = scores[slots:keys]
        theirs = segcol[pl.ds(pl.multiple_of(shard * block, block), block), 0:1]
        fresh = jnp.where(theirs <= asks, fresh, -jnp.inf)
        masked = jnp.concatenate([old, fresh], axis=0)
        peak = jnp.max(masked, axis=0, keepdims=True)
        expo = jnp.exp2((masked - peak) * c2)
        total = jnp.sum(expo, axis=0, keepdims=True)
        mixed = lax.dot_general(
            kv[r, 1], expo.astype(jnp.bfloat16), (((0,), (0,)), ((), ())),
            preferred_element_type=jnp.float32)
        if r == 0:
            top, denom, numer = peak, total, mixed
        else:
            before = run[u, 0:1]
            top = jnp.maximum(before, peak)
            keep, add = jnp.exp2((before - top) * c2), jnp.exp2((peak - top) * c2)
            denom = run[u, 1:2] * keep + total * add
            numer = acc[u] * keep + mixed * add
        if r < GANG - 1:
            run[u, 0:1], run[u, 1:2] = top, denom
            acc[u] = numer
        else:
            most = jnp.maximum(jnp.max(jnp.abs(numer), axis=0, keepdims=True), TINY)
            level = jnp.round(numer * (STEPS / most))
            rows = level.T.astype(jnp.int32).astype(jnp.int16).reshape(group, T, R, hd)
            for k in range(group):
                j = u * group + k
                osend[j] = rows[k]
                stats = [x[:, k * B:(k + 1) * B] for x in (top, denom, most)]
                ssend[j] = jnp.concatenate(stats + stats[:1] * 5, axis=0)
                for i in range(T):
                    if j or i:
                        s_copy(j, i).start()
                        o_copy(j, i).start()
    orecv[0, me] = osend[0, me]
    srecv[0, me] = ssend[0]
    for j in range(H):
        for i in range(T):
            if j or i:
                s_arrival(j, i).wait_recv()
                o_arrival(j, i).wait_recv()
    for g in range(T):
        tops = [srecv[j, g, 0:1] for j in range(H)]
        top = functools.reduce(jnp.maximum, tops)
        ws = [jnp.exp2((x - top) * c2) for x in tops]
        total = sum(w * srecv[j, g, 1:2] for j, w in enumerate(ws))
        lsebuf[g] = jnp.broadcast_to(top * scale + jnp.log(total), (8, B))
        inverse = 1.0 / (total * STEPS)
        ws = [w * srecv[j, g, 2:3] * inverse for j, w in enumerate(ws)]
        ws += [jnp.zeros_like(top)] * (-H % 8)
        wcol[...] = jnp.concatenate(ws, axis=0).T
        cols = wcol[pl.ds(me * R, R), :]
        final = sum(
            cols[:, j:j + 1] * orecv[j, g].astype(jnp.int32).astype(jnp.float32) for j in range(H))
        first = g * heads * hd
        out_ref[:, first:first + heads * hd] = jnp.concatenate(
            [final[h * tokens:(h + 1) * tokens] for h in range(heads)], axis=1).astype(out_ref.dtype)
    spot = lax.broadcasted_iota(jnp.int32, (heads, B), 1)
    row = lax.broadcasted_iota(jnp.int32, (heads, B), 0)
    spread = jnp.where(lax.div(lax.rem(spot, jnp.int32(R)), jnp.int32(tokens)) == row, lsebuf[me, 0:1], 0.0)
    spot = lax.broadcasted_iota(jnp.int32, (block, B), 1)
    row = lax.broadcasted_iota(jnp.int32, (block, B), 0)
    pick = lax.div(spot, jnp.int32(R)) * tokens + lax.rem(spot, jnp.int32(tokens)) == row
    lse_ref[...] = lax.dot_general(
        spread, pick.astype(jnp.float32), (((1,), (1,)), ((), ())),
        precision=lax.Precision.HIGHEST, preferred_element_type=jnp.float32)
    for j in range(H):
        for i in range(T):
            if j or i:
                q_copy(j, i).wait_send()
                s_copy(j, i).wait_send()
                o_copy(j, i).wait_send()
    for copy in far + near + relay:
        copy.wait_send()


def hand_over(out_ref, lse_ref, out_to, lse_to, sems):
    copies = [
        pltpu.make_async_copy(out_ref, out_to, sems.at[0]),
        pltpu.make_async_copy(lse_ref, lse_to, sems.at[1]),
    ]
    for copy in copies:
        copy.start()
    for copy in copies:
        copy.wait()


def shards(q_new, kv_new, kv_cache, cache_lens, segment_ids):
    hd = kv_cache.shape[2]
    block, slots = kv_new.shape[1], kv_cache.shape[1]
    tokens = q_new.shape[0]
    n, T = lax.axis_size("ctx"), lax.axis_size("tp")
    H = n // GANG
    heads = q_new.shape[1] // (hd * T)
    R = tokens * heads
    B = T * R
    hpad = H + (-H % 8)
    vmem = pl.BlockSpec(memory_space=pltpu.VMEM)
    hbm = pl.BlockSpec(memory_space=pltpu.HBM)
    group = 2 if H % 2 == 0 else 1
    new = segment_ids.shape[0]
    dma = pltpu.SemaphoreType.DMA
    out, lse = pl.pallas_call(
        functools.partial(kernel, H, T, R, hd ** -0.5),
        out_shape=(
            jax.ShapeDtypeStruct(q_new.shape, jnp.bfloat16),
            jax.ShapeDtypeStruct((heads, block), jnp.float32),
        ),
        in_specs=[hbm] * 5,
        out_specs=(vmem, vmem),
        scratch_shapes=[
            pltpu.VMEM(q_new.shape, jnp.bfloat16),
            pltpu.VMEM((T, R, hd), jnp.bfloat16),
            pltpu.SMEM(cache_lens.shape, jnp.int32),
            pltpu.VMEM((1, new), jnp.int32),
            pltpu.VMEM((new, 8), jnp.float32),
            pltpu.VMEM((H, B), jnp.float32),
            pltpu.VMEM((H, T, R, hd), jnp.bfloat16),
            pltpu.VMEM((GANG, 2, slots + block, hd), jnp.bfloat16),
            pltpu.VMEM((H, T, R, hd), jnp.int16),
            pltpu.VMEM((H, T, R, hd), jnp.int16),
            pltpu.VMEM((H, 8, B), jnp.float32),
            pltpu.VMEM((H, T, 8, B), jnp.float32),
            pltpu.VMEM((H // group, hd, group * B), jnp.float32),
            pltpu.VMEM((H // group, 8, group * B), jnp.float32),
            pltpu.VMEM((B, hpad), jnp.float32),
            pltpu.VMEM((T, 8, B), jnp.float32),
            dma((H, T)), dma((H, T)), dma((GANG, 2)), dma((GANG, 2)), dma((5,)), dma((H, T)), dma((H, T)), dma((H, T)), dma((H, T)),
        ],
        compiler_params=pltpu.CompilerParams(
            collective_id=0, has_side_effects=True, vmem_limit_bytes=60 * 2 ** 20),
    )(q_new, kv_cache, kv_new, cache_lens, segment_ids.reshape(1, new))
    out, lse = pl.pallas_call(
        hand_over,
        out_shape=(jax.ShapeDtypeStruct(out.shape, out.dtype), jax.ShapeDtypeStruct(lse.shape, lse.dtype)),
        in_specs=[hbm] * 2,
        out_specs=(hbm, hbm),
        scratch_shapes=[dma((2,))],
        compiler_params=pltpu.CompilerParams(vmem_limit_bytes=60 * 2 ** 20),
    )(out, lse)
    return out, lse.T


def solution(mesh):
    return jax.shard_map(
        shards,
        mesh=mesh,
        in_specs=(P(("ctx", "tp"), None), P(None, "ctx", "tp"), P(None, "ctx", "tp"), P(), P()),
        out_specs=(P(("ctx", "tp"), None), P("ctx", "tp")),
        check_vma=False,
    )
```

```python
import functools
import math

import jax
import jax.numpy as jnp
from jax import lax
from jax.experimental import pallas as pl
from jax.experimental.pallas import tpu as pltpu
from jax.sharding import PartitionSpec as P

TINY, STEPS = 1e-30, 32767.0
GANG = 4


def kernel(
    H, T, R, scale,
    q_hbm, cache_ref, new_ref, lens_hbm, seg_hbm,
    out_ref, lse_ref,
    qraw, q_ref, lens_ref, segrow, segcol, qseg,
    qbuf, kv, osend, orecv, ssend, srecv, acc, run, wcol, lsebuf,
    q_send, q_recv, kv_send, kv_recv, own_sem, o_send, o_recv, s_send, s_recv,
):
    c2 = scale * math.log2(math.e)
    ctx, me = lax.axis_index("ctx"), lax.axis_index("tp")
    hi, lo = ctx // GANG, lax.rem(ctx, GANG)
    base = hi * GANG
    b0, b1 = lax.rem(lo, 2), lo // 2
    flip = [b1 * 2 + b0, b1 * 2 + 1 - b0, (1 - b1) * 2 + b0, (1 - b1) * 2 + 1 - b0]
    slots, block = cache_ref.shape[1], new_ref.shape[1]
    keys = slots + block
    tokens, hd = qraw.shape[0], cache_ref.shape[2]
    heads, B = R // tokens, T * R

    def dev(c, t):
        return {"ctx": c, "tp": t}

    def peer(j):
        return lax.rem(hi + j + H, H) * GANG + lo

    def tpeer(i):
        return lax.rem(me + i + T, T)

    barrier = pltpu.get_barrier_semaphore()
    count = 0
    for j in range(H):
        for i in range(T):
            if j or i:
                pl.semaphore_signal(barrier, inc=1, device_id=dev(peer(j), tpeer(i)))
                count += 1
    for r in (1, 2):
        pl.semaphore_signal(barrier, inc=1, device_id=dev(base + flip[r], me))
        count += 1
    local = [
        pltpu.make_async_copy(q_hbm, qraw, own_sem.at[0]),
        pltpu.make_async_copy(seg_hbm, segrow, own_sem.at[1]),
        pltpu.make_async_copy(lens_hbm, lens_ref, own_sem.at[2]),
        pltpu.make_async_copy(new_ref, kv.at[0, :, slots:keys], own_sem.at[3]),
        pltpu.make_async_copy(cache_ref, kv.at[0, :, 0:slots], own_sem.at[4]),
    ]
    for copy in local:
        copy.start()
    local[0].wait()
    for g in range(T):
        first = g * heads * hd
        wide = qraw[:, first:first + heads * hd].astype(jnp.float32)
        q_ref[g] = jnp.concatenate(
            [wide[:, h * hd:(h + 1) * hd] for h in range(heads)], axis=0).astype(jnp.bfloat16)
    local[1].wait()
    total_new = segrow.shape[1]
    segcol[...] = jnp.broadcast_to(segrow[...].astype(jnp.float32), (8, total_new)).T
    lane = lax.broadcasted_iota(jnp.int32, (1, B), 1)
    inside = lax.div(lane, jnp.int32(R)) * tokens + lax.rem(lane, jnp.int32(tokens))
    token = lax.broadcasted_iota(jnp.int32, (total_new, B), 0)
    for j in range(H):
        here = token == inside + peer(j) * block
        qseg[j:j + 1] = jnp.sum(jnp.where(here, segcol[:, 0:1], 0.0), axis=0, keepdims=True)
    for copy in local[2:]:
        copy.wait()
    pl.semaphore_wait(barrier, count)

    def q_copy(j, i):
        g = tpeer(i)
        return pltpu.make_async_remote_copy(
            q_ref.at[g], qbuf.at[j, me], q_send.at[j, i], q_recv.at[j, i],
            device_id=dev(peer(-j), g))

    def q_arrival(j, i):
        return pltpu.make_async_remote_copy(
            q_ref.at[me], qbuf.at[j, tpeer(-i)], q_send.at[j, i], q_recv.at[j, i],
            device_id=dev(peer(j), tpeer(-i)))

    def kv_copy(source, slot, part, hop):
        return pltpu.make_async_remote_copy(
            kv.at[source, part], kv.at[slot, part], kv_send.at[slot, part], kv_recv.at[slot, part],
            device_id=dev(base + flip[hop], me))

    far = [kv_copy(0, 2, part, 2) for part in range(2)]
    near = [kv_copy(0, 1, part, 1) for part in range(2)]
    relay = [kv_copy(2, 3, part, 1) for part in range(2)]
    for j in range(H):
        for i in range(T):
            if j or i:
                q_copy(j, i).start()
    for copy in far + near:
        copy.start()
    qbuf[0, me] = q_ref[me]
    for j in range(H):
        for i in range(T):
            if j or i:
                q_arrival(j, i).wait_recv()

    def o_copy(j, i):
        t = tpeer(i)
        return pltpu.make_async_remote_copy(
            osend.at[j, t], orecv.at[j, me], o_send.at[j, i], o_recv.at[j, i],
            device_id=dev(peer(j), t))

    def o_arrival(j, i):
        return pltpu.make_async_remote_copy(
            osend.at[j, me], orecv.at[j, tpeer(-i)], o_send.at[j, i], o_recv.at[j, i],
            device_id=dev(peer(-j), tpeer(-i)))

    def s_copy(j, i):
        return pltpu.make_async_remote_copy(
            ssend.at[j], srecv.at[j, me], s_send.at[j, i], s_recv.at[j, i],
            device_id=dev(peer(j), tpeer(i)))

    def s_arrival(j, i):
        return pltpu.make_async_remote_copy(
            ssend.at[j], srecv.at[j, tpeer(-i)], s_send.at[j, i], s_recv.at[j, i],
            device_id=dev(peer(-j), tpeer(-i)))

    group = 2 if H % 2 == 0 else 1
    width = group * B
    units = H // group
    order = [(r, u) for r in (0, 1) for u in range(units)] + [(r, u) for u in range(units) for r in (2, 3)]
    for r, u in order:
        if u == 0:
            if r == 1:
                for copy in near:
                    copy.wait_recv()
            if r == 2:
                for copy, onward in zip(far, relay):
                    copy.wait_recv()
                    onward.start()
            if r == 3:
                for copy in relay:
                    copy.wait_recv()
        shard = base + flip[r]
        filled = lens_ref[shard]
        queries = qbuf[u * group:(u + 1) * group].reshape(width, q_ref.shape[2])
        asks = jnp.concatenate(
            [qseg[u * group + k:u * group + k + 1] for k in range(group)], axis=1)
        scores = lax.dot_general(
            kv[r, 0], queries, (((1,), (1,)), ((), ())), preferred_element_type=jnp.float32)
        old = scores[0:slots]
        spot = lax.broadcasted_iota(jnp.int32, old.shape, 0)
        old = jnp.where(spot < filled, old, -jnp.inf)
        fresh = scores[slots:keys]
        theirs = segcol[pl.ds(pl.multiple_of(shard * block, block), block), 0:1]
        fresh = jnp.where(theirs <= asks, fresh, -jnp.inf)
        masked = jnp.concatenate([old, fresh], axis=0)
        peak = jnp.max(masked, axis=0, keepdims=True)
        expo = jnp.exp2((masked - peak) * c2)
        total = jnp.sum(expo, axis=0, keepdims=True)
        mixed = lax.dot_general(
            kv[r, 1], expo.astype(jnp.bfloat16), (((0,), (0,)), ((), ())),
            preferred_element_type=jnp.float32)
        if r == 0:
            top, denom, numer = peak, total, mixed
        else:
            before = run[u, 0:1]
            top = jnp.maximum(before, peak)
            keep, add = jnp.exp2((before - top) * c2), jnp.exp2((peak - top) * c2)
            denom = run[u, 1:2] * keep + total * add
            numer = acc[u] * keep + mixed * add
        if r < GANG - 1:
            run[u, 0:1], run[u, 1:2] = top, denom
            acc[u] = numer
        else:
            most = jnp.maximum(jnp.max(jnp.abs(numer), axis=0, keepdims=True), TINY)
            level = jnp.round(numer * (STEPS / most))
            rows = level.T.astype(jnp.int32).astype(jnp.int16).reshape(group, T, R, hd)
            for k in range(group):
                j = u * group + k
                osend[j] = rows[k]
                stats = [x[:, k * B:(k + 1) * B] for x in (top, denom, most)]
                ssend[j] = jnp.concatenate(stats + stats[:1] * 5, axis=0)
                for i in range(T):
                    if j or i:
                        s_copy(j, i).start()
                        o_copy(j, i).start()
    orecv[0, me] = osend[0, me]
    srecv[0, me] = ssend[0]
    for j in range(H):
        for i in range(T):
            if j or i:
                s_arrival(j, i).wait_recv()
                o_arrival(j, i).wait_recv()
    for g in range(T):
        tops = [srecv[j, g, 0:1] for j in range(H)]
        top = functools.reduce(jnp.maximum, tops)
        ws = [jnp.exp2((x - top) * c2) for x in tops]
        total = sum(w * srecv[j, g, 1:2] for j, w in enumerate(ws))
        lsebuf[g] = jnp.broadcast_to(top * scale + jnp.log(total), (8, B))
        inverse = 1.0 / (total * STEPS)
        ws = [w * srecv[j, g, 2:3] * inverse for j, w in enumerate(ws)]
        ws += [jnp.zeros_like(top)] * (-H % 8)
        wcol[...] = jnp.concatenate(ws, axis=0).T
        cols = wcol[pl.ds(me * R, R), :]
        final = sum(
            cols[:, j:j + 1] * orecv[j, g].astype(jnp.int32).astype(jnp.float32) for j in range(H))
        first = g * heads * hd
        out_ref[:, first:first + heads * hd] = jnp.concatenate(
            [final[h * tokens:(h + 1) * tokens] for h in range(heads)], axis=1).astype(out_ref.dtype)
    spot = lax.broadcasted_iota(jnp.int32, (heads, B), 1)
    row = lax.broadcasted_iota(jnp.int32, (heads, B), 0)
    spread = jnp.where(lax.div(lax.rem(spot, jnp.int32(R)), jnp.int32(tokens)) == row, lsebuf[me, 0:1], 0.0)
    spot = lax.broadcasted_iota(jnp.int32, (block, B), 1)
    row = lax.broadcasted_iota(jnp.int32, (block, B), 0)
    pick = lax.div(spot, jnp.int32(R)) * tokens + lax.rem(spot, jnp.int32(tokens)) == row
    lse_ref[...] = lax.dot_general(
        spread, pick.astype(jnp.float32), (((1,), (1,)), ((), ())),
        precision=lax.Precision.HIGHEST, preferred_element_type=jnp.float32)
    for j in range(H):
        for i in range(T):
            if j or i:
                q_copy(j, i).wait_send()
                s_copy(j, i).wait_send()
                o_copy(j, i).wait_send()
    for copy in far + near + relay:
        copy.wait_send()


def hand_over(out_ref, lse_ref, out_to, lse_to):
    out_to[...] = out_ref[...]
    lse_to[...] = lse_ref[...]


def shards(q_new, kv_new, kv_cache, cache_lens, segment_ids):
    hd = kv_cache.shape[2]
    block, slots = kv_new.shape[1], kv_cache.shape[1]
    tokens = q_new.shape[0]
    n, T = lax.axis_size("ctx"), lax.axis_size("tp")
    H = n // GANG
    heads = q_new.shape[1] // (hd * T)
    R = tokens * heads
    B = T * R
    hpad = H + (-H % 8)
    vmem = pl.BlockSpec(memory_space=pltpu.VMEM)
    hbm = pl.BlockSpec(memory_space=pltpu.HBM)
    group = 2 if H % 2 == 0 else 1
    new = segment_ids.shape[0]
    dma = pltpu.SemaphoreType.DMA
    out, lse = pl.pallas_call(
        functools.partial(kernel, H, T, R, hd ** -0.5),
        out_shape=(
            jax.ShapeDtypeStruct(q_new.shape, jnp.bfloat16),
            jax.ShapeDtypeStruct((heads, block), jnp.float32),
        ),
        in_specs=[hbm] * 5,
        out_specs=(vmem, vmem),
        scratch_shapes=[
            pltpu.VMEM(q_new.shape, jnp.bfloat16),
            pltpu.VMEM((T, R, hd), jnp.bfloat16),
            pltpu.SMEM(cache_lens.shape, jnp.int32),
            pltpu.VMEM((1, new), jnp.int32),
            pltpu.VMEM((new, 8), jnp.float32),
            pltpu.VMEM((H, B), jnp.float32),
            pltpu.VMEM((H, T, R, hd), jnp.bfloat16),
            pltpu.VMEM((GANG, 2, slots + block, hd), jnp.bfloat16),
            pltpu.VMEM((H, T, R, hd), jnp.int16),
            pltpu.VMEM((H, T, R, hd), jnp.int16),
            pltpu.VMEM((H, 8, B), jnp.float32),
            pltpu.VMEM((H, T, 8, B), jnp.float32),
            pltpu.VMEM((H // group, hd, group * B), jnp.float32),
            pltpu.VMEM((H // group, 8, group * B), jnp.float32),
            pltpu.VMEM((B, hpad), jnp.float32),
            pltpu.VMEM((T, 8, B), jnp.float32),
            dma((H, T)), dma((H, T)), dma((GANG, 2)), dma((GANG, 2)), dma((5,)), dma((H, T)), dma((H, T)), dma((H, T)), dma((H, T)),
        ],
        compiler_params=pltpu.CompilerParams(
            collective_id=0, has_side_effects=True, vmem_limit_bytes=60 * 2 ** 20),
    )(q_new, kv_cache, kv_new, cache_lens, segment_ids.reshape(1, new))
    out, lse = pl.pallas_call(
        hand_over,
        out_shape=(jax.ShapeDtypeStruct(out.shape, out.dtype), jax.ShapeDtypeStruct(lse.shape, lse.dtype)),
        in_specs=[vmem] * 2,
        out_specs=(vmem, vmem),
        compiler_params=pltpu.CompilerParams(vmem_limit_bytes=60 * 2 ** 20),
    )(out, lse)
    return out, lse.T


def solution(mesh):
    return jax.shard_map(
        shards,
        mesh=mesh,
        in_specs=(P(("ctx", "tp"), None), P(None, "ctx", "tp"), P(None, "ctx", "tp"), P(), P()),
        out_specs=(P(("ctx", "tp"), None), P("ctx", "tp")),
        check_vma=False,
    )
```
